32 devices in a mesh: groups: 2 (over x), blk: 8 (over z, y), rep: 2 (over core).
Axes of the slice: x: 2, y: 2, z: 4, core: 2. Of those that a mesh axis runs over, the one named last changes fastest.
Arguments:
- frames: bfloat16 [65536, 64], P(('groups', 'blk')), parts along dimension 0, may hold values from -6 to 6
- degree: float32 [65536], P(('groups', 'blk')), parts along dimension 0, may hold values from 1 to 16
- start: float32 [65536, 64], P(('groups', 'blk')), parts along dimension 0, may hold values from -6 to 6
- block_slot: int32 [64], P('groups'), parts along dimension 0, may hold values from 0 to 31, as said below
- pair_list: int32 [16, 2, 4, 2], P(('groups', 'blk'), 'rep'), parts along dimension 0, may hold values from 0 to 31, as said below
- pair_count: int32 [16, 2], P(('groups', 'blk'), 'rep'), parts along dimension 0, may hold values from 3 to 4, as said below
Outputs:
- subspace: float32 [65536, 64], P(('groups', 'blk', 'rep')), parts along dimension 0
- factor: float32 [128, 64], P('groups'), parts along dimension 0
The draws below stay inside these ranges and needn't reach their ends.
There are 2 independent parts, one for each index of `groups`. The reference program is written for one: setup_inputs(seed, part) draws one part's arguments, and reference() takes and returns one part's arrays. A program takes and returns all parts, laid end to end along the dimension named above; each array names one. Nothing has to cross between parts.
Inputs may be any that keep to these rules, and one draw needn't show every extreme that they name: `block_slot`: A permutation of the 32 storage slots; slot s lies on blk index s // 4. Every row block of pair_list[i] sits at a storage slot on blk index i. Over the two halves of one owner, all 8 slots, live or not, name column blocks on different blk indices. Slots beyond pair_count are ignored. A pair may be listed more than once over all owners; each listing adds its tile. `pair_count`: counts differ from device to device.
All inputs are finite; a program needn't handle non-finite values.
Results may differ from the reference program's by a relative error of at most 0.0091.
Values may be sent and summed in bfloat16 or wider, within the bound.
A program may use at most 128 MiB of HBM per device.

```python
import math
import jax
import jax.numpy as jnp
from jax import lax

BS = 1024
D_CV = 64
K = 64
BLK_DEV = 4
ITERS = 2
PSLOT = 4
NB = 32
NF = 32768
N_BLK = 8
N_REP = 2


def shared_slots(key):
    return jax.random.permutation(key, NB).astype(jnp.int32)


def draw_block_slot(key, part):
    return shared_slots(key)


def draw_pair_list(key, part):
    slot_of = shared_slots(key)
    block_at = jnp.argsort(slot_of, stable=True).astype(jnp.int32)
    key = jax.random.fold_in(key, 7)
    common = jax.random.randint(jax.random.fold_in(key, 0), (), 0, N_BLK).astype(jnp.int32)

    def owner_list(owner):
        owner_key = jax.random.fold_in(key, owner + 1)
        others = jax.random.permutation(jax.random.fold_in(owner_key, 0), N_BLK - 1).astype(jnp.int32)
        others = others + (others >= common).astype(jnp.int32)
        peer = jnp.concatenate([common.reshape(1), others])[:2 * PSLOT]
        col_local = jax.random.randint(jax.random.fold_in(owner_key, 1), (2 * PSLOT,), 0, BLK_DEV).astype(jnp.int32)
        row_local = jax.random.randint(jax.random.fold_in(owner_key, 2), (2 * PSLOT,), 0, BLK_DEV).astype(jnp.int32)
        col_block = block_at[peer * BLK_DEV + col_local]
        row_block = block_at[owner * BLK_DEV + row_local]
        return jnp.stack([row_block, col_block], axis=1).reshape(N_REP, PSLOT, 2)
    return jax.vmap(owner_list)(jnp.arange(N_BLK, dtype=jnp.int32)).astype(jnp.int32)


def draw_pair_count(key, part):
    key = jax.random.fold_in(key, 5)
    lowest = PSLOT - PSLOT // 4
    counts = jax.random.randint(jax.random.fold_in(key, 0), (N_BLK * N_REP,), lowest, PSLOT + 1).astype(jnp.int32)
    fullest = jax.random.randint(jax.random.fold_in(key, 1), (), 0, N_BLK * N_REP)
    lightest = (fullest + 1 + jax.random.randint(jax.random.fold_in(key, 2), (), 0, N_BLK * N_REP - 1)) % (N_BLK * N_REP)
    counts = jnp.where(jnp.arange(N_BLK * N_REP) == fullest, PSLOT, counts)
    counts = jnp.where(jnp.arange(N_BLK * N_REP) == lightest, lowest, counts)
    return counts.reshape(N_BLK, N_REP).astype(jnp.int32)


def levels(rng, dims, pieces, low, largest):
    loudness, own = 1.0, jax.random.fold_in(rng, 6)
    for dim, shards_of in pieces:
        steps = jnp.exp(jax.random.uniform(jax.random.fold_in(own, dim), (shards_of,), jnp.float32, low / len(pieces), largest / len(pieces)))
        loudness = loudness * jnp.repeat(steps, dims[dim] // shards_of).reshape([-1 if axis == dim else 1 for axis in range(len(dims))])
    return loudness


def normal_values(key, dims, deviation, reach, cuts=(), held_as=jnp.bfloat16):
    array = jax.random.normal(key, dims, jnp.float32) * deviation
    if len(cuts) > 0:
        array = levels(key, dims, cuts, -0.22, 0.18) * array
    return jnp.clip(array, min=-reach, max=reach).astype(held_as)


def setup_inputs(seed: int = 0, part: int = 0) -> dict:
    key_of = jax.random.split(jax.random.key(seed), 7)
    part_keys = jax.random.split(jax.random.fold_in(key_of[6], part), 7)
    frames = normal_values(part_keys[0], (NF, D_CV), 1.0, 6.0, ((0, 8),))
    degree = jnp.clip(jnp.exp(math.log(16.0) - 2.7725887 * jax.random.uniform(part_keys[1], (NF,), jnp.float32) ** levels(part_keys[1], (NF,), ((0, 8),), -0.2, 0.2)), 1.0, 16.0)
    start = normal_values(part_keys[2], (NF, K), 1.0, 6.0, ((0, 8),), jnp.float32)
    block_slot = draw_block_slot(jax.random.fold_in(jax.random.fold_in(key_of[6], part), 71), part)
    pair_list = draw_pair_list(jax.random.fold_in(jax.random.fold_in(key_of[6], part), 71), part)
    pair_count = draw_pair_count(jax.random.fold_in(jax.random.fold_in(key_of[6], part), 71), part)
    return dict(frames=frames, degree=degree, start=start, block_slot=block_slot, pair_list=pair_list, pair_count=pair_count)


def gauss_tile(left, right):
    left_sq = lax.optimization_barrier(jnp.sum(jnp.square(left.astype(jnp.float32)), axis=1))
    right_sq = lax.optimization_barrier(jnp.sum(jnp.square(right.astype(jnp.float32)), axis=1))
    cross = lax.dot_general(left.astype(jnp.float32), right.astype(jnp.float32), (((1,), (1,)), ((), ())), preferred_element_type=jnp.float32)
    dist = left_sq[:, None] + right_sq[None, :] - 2.0 * cross
    return jnp.exp(-dist * (4.0 / D_CV)).astype(jnp.bfloat16)

def reference(frames, degree, start, block_slot, pair_list, pair_count):
    frame_blocks = frames.reshape(NB, BS, D_CV)
    scale = lax.rsqrt(degree).reshape(NB, BS, 1)
    flat_pairs = pair_list.reshape(-1, 2)
    live = (jnp.arange(PSLOT, dtype=jnp.int32)[None, None, :] < pair_count[:, :, None]).reshape(-1)
    row_slot = block_slot[flat_pairs[:, 0]].astype(jnp.int32)
    col_slot = block_slot[flat_pairs[:, 1]].astype(jnp.int32)
    total_pairs = flat_pairs.shape[0]
    vectors = start
    factor = jnp.zeros((K, K), jnp.float32)
    for step in range(ITERS):
        scaled = (vectors.reshape(NB, BS, K) * scale).astype(jnp.bfloat16)

        def add_pair(sums, index):
            here = row_slot[index]
            there = col_slot[index]
            tile = gauss_tile(frame_blocks[here], frame_blocks[there])
            forward = jnp.dot(tile.astype(jnp.float32), scaled[there].astype(jnp.float32), preferred_element_type=jnp.float32)
            sums = sums.at[here].add(forward)
            backward = lax.dot_general(tile.astype(jnp.float32), scaled[here].astype(jnp.float32), (((0,), (0,)), ((), ())), preferred_element_type=jnp.float32)
            backward = backward.astype(jnp.bfloat16).astype(jnp.float32)
            backward = jnp.where(here != there, backward, jnp.zeros_like(backward))
            return sums.at[there].add(backward)

        def one_pair(index, sums):
            return lax.cond(live[index], lambda current: add_pair(current, index), lambda current: current, sums)
        sums = lax.fori_loop(0, total_pairs, one_pair, jnp.zeros((NB, BS, K), jnp.float32))
        mapped = (sums * scale).reshape(NF, K)
        gram = lax.dot_general(mapped.astype(jnp.float32), mapped.astype(jnp.float32), (((0,), (0,)), ((), ())), precision=lax.Precision.HIGHEST, preferred_element_type=jnp.float32) / NF
        factor = jnp.linalg.cholesky(gram)
        vectors = jax.scipy.linalg.solve_triangular(factor, mapped.T, lower=True).T
    return (vectors, factor)
```

```python
import functools

import jax
import jax.numpy as jnp
from jax import lax
from jax.experimental import pallas as pl
from jax.experimental.pallas import tpu as pltpu
from jax.sharding import PartitionSpec as P

BS = 1024
ITERS = 2
HALF = BS // 2
QTR = BS // 4
DEAD = 100000
MESH = pl.DeviceIdType.MESH
F32 = jnp.float32
BF16 = jnp.bfloat16
HI = lax.Precision.HIGHEST
NN = ((1,), (0,))
NT = ((1,), (1,))
TN = ((0,), (0,))


def mm(a, b, dims, precision=None):
    return lax.dot_general(
        a, b, (dims, ((), ())), precision=precision, preferred_element_type=F32
    )


def rows_cols(shape):
    return (
        lax.broadcasted_iota(jnp.int32, shape, 0),
        lax.broadcasted_iota(jnp.int32, shape, 1),
    )


def flags(cond, dtype=BF16):
    return jnp.where(cond, 1.0, 0.0).astype(dtype)


def cholesky_and_inverse(gram, n):
    rows, cols = rows_cols((n, 2 * n))
    a = jnp.where(cols < n, gram, flags(cols == rows + n, F32))
    row_id = lax.broadcasted_iota(jnp.int32, (n, 1), 0)
    for j in range(n - 1):
        col = jnp.sum(jnp.where(cols == j, a, 0.0), axis=1, keepdims=True)
        mult = jnp.where(row_id > j, col, 0.0) / col[j : j + 1, :]
        a = a - mult * a[j : j + 1, :]
    diag = jnp.sum(jnp.where(cols == rows, a, 0.0), axis=1, keepdims=True)
    return a * lax.rsqrt(diag)


def kernel(
    peers, blocks, width, slots, total_rows,
    frames, degree, start, block_slot, pairs, count,
    out, factor,
    info, table, fw, yw, scale, fsend, frecv, ysend, yrecv, fa, q, rhs, z, zs,
    bsend, brecv, eb, zx1, zx2, gx, chol,
    info_s, info_r, table_s, fs, fr, ys, yr, bs, br, zsem_s, zsem_r, gs, gr, yos, yor,
):
    me = lax.axis_index("blk")
    r = lax.axis_index("rep")
    k = 2 * me + r
    devs = 2 * peers
    per = peers // 2
    lanes = blocks * width

    def dev(kk):
        return {"blk": kk // 2, "rep": lax.rem(kk, 2)}

    barrier = pltpu.get_barrier_semaphore()

    def greet(t, _):
        pl.semaphore_signal(
            barrier, inc=1, device_id=dev(lax.rem(k + t, devs)), device_id_type=MESH
        )
        return 0

    lax.fori_loop(1, devs, greet, 0)

    lane = lax.broadcasted_iota(jnp.int32, (1, 128), 1)
    mine = jnp.zeros((1, 128), jnp.int32)
    live_count = count[0]
    for s in range(slots):
        mine = jnp.where(lane == s, block_slot[pairs[2 * s]], mine)
        mine = jnp.where(lane == 16 + s, block_slot[pairs[2 * s + 1]], mine)
        mine = jnp.where(lane == 32 + s, jnp.where(s < live_count, 1, 0), mine)
    info[k] = mine

    sel_r, sel_c = rows_cols((width, lanes))
    acc = jnp.zeros((BS, lanes), F32)
    for b in range(blocks):
        acc = acc + mm(frames[b * BS : (b + 1) * BS, :], flags(sel_c == sel_r + b * width), NN)
    fw[...] = acc.astype(BF16)

    pl.semaphore_wait(barrier, devs - 1)

    def info_copy(t, src):
        return pltpu.make_async_remote_copy(
            src_ref=info.at[src], dst_ref=info.at[src],
            send_sem=info_s.at[t], recv_sem=info_r.at[src],
            device_id=dev(lax.rem(k + t, devs)), device_id_type=MESH,
        )

    def info_send(t, _):
        info_copy(t, k).start()
        return 0

    lax.fori_loop(1, devs, info_send, 0)

    gr_r, gr_c = rows_cols((blocks, lanes))
    spread = flags(gr_c // width == gr_r, F32)
    scale[...] = lax.rsqrt(mm(degree[...], spread, TN, HI))
    acc = jnp.zeros((BS, lanes), F32)
    for b in range(blocks):
        acc = acc + mm(
            start[b * BS : (b + 1) * BS, :], flags(sel_c == sel_r + b * width, F32), NN, HI
        )
    yw[0] = (acc * scale[...]).astype(BF16)

    def info_wait(t, _):
        info_copy(t, lax.rem(k + t, devs)).wait_recv()
        return 0

    lax.fori_loop(1, devs, info_wait, 0)
    to_table = pltpu.make_async_copy(info, table, table_s)
    to_table.start()
    to_table.wait()

    def entries(owner):
        for half in range(2):
            for s in range(slots):
                row = table[2 * owner + half, 0, s]
                col = table[2 * owner + half, 0, 16 + s]
                alive = table[2 * owner + half, 0, 32 + s]
                yield row, col, alive

    def asked(d):
        low = me * blocks
        found = jnp.int32(-DEAD)
        for _, col, alive in entries(lax.rem(me + d, peers)):
            hit = (col >= low) & (col < low + blocks) & (alive == 1)
            found = found + jnp.where(hit, col - low + DEAD, 0)
        return found

    def own(d, skip_equal):
        low = lax.rem(me - d + peers, peers) * blocks
        found = jnp.int32(-DEAD)
        for row, col, alive in entries(me):
            hit = (col >= low) & (col < low + blocks) & (alive == 1)
            if skip_equal:
                hit = hit & (row != col)
            found = found + jnp.where(hit, row - me * blocks + DEAD, 0)
        return found

    pk_r, pk_c = rows_cols((lanes, 2 * width))

    def pack(source, it, first, block):
        top = pl.multiple_of(first, HALF)
        upper = source(pl.ds(top, QTR))
        lower = source(pl.ds(pl.multiple_of(top + QTR, QTR), QTR))
        want = pk_r - block * width
        got = mm(upper, flags((want == pk_c) & (pk_c < width)), NN)
        got = got + mm(lower, flags((want == pk_c - width) & (pk_c >= width)), NN)
        return got.astype(BF16)

    def block_copy(send, recv, ssem, rsem, d, half):
        return pltpu.make_async_remote_copy(
            src_ref=send.at[d], dst_ref=recv.at[d // 2, half],
            send_sem=ssem.at[d], recv_sem=rsem.at[d // 2, half],
            device_id={"blk": lax.rem(me + d, peers), "rep": lax.rem(d, 2)},
            device_id_type=MESH,
        )

    def send_blocks(source, it, send, recv, ssem, rsem):
        def one(d, _):
            send[d] = pack(source, it, r * HALF, asked(d))
            block_copy(send, recv, ssem, rsem, d, r).start()
            return 0

        lax.fori_loop(1, peers, one, 0)

    def fill_own(source, recv):
        @pl.when(r == 0)
        def _():
            block = asked(0)
            for half in range(2):
                recv[0, half] = pack(source, 0, half * HALF, block)

    def wait_blocks(m, send, recv, ssem, rsem):
        @pl.when(2 * m + r != 0)
        def _():
            for half in range(2):
                pltpu.make_async_remote_copy(
                    src_ref=send.at[0], dst_ref=recv.at[m, half],
                    send_sem=ssem.at[0], recv_sem=rsem.at[m, half],
                    device_id={"blk": me, "rep": 1 - r}, device_id_type=MESH,
                ).wait_recv()

    def from_fw(idx):
        return fw[idx, :]

    send_blocks(from_fw, 0, fsend, frecv, fs, fr)
    fill_own(from_fw, frecv)
    send_blocks(lambda idx: yw[0, idx, :], 0, ysend.at[0], yrecv.at[0], ys.at[0], yr.at[0])

    on_r, on_c = rows_cols((8, 2 * width))
    ones8 = flags(on_c // width == on_r, F32) * (1.0 / 16.0)

    def make_tile(m, _):
        block = own(2 * m + r, False)
        want = pk_r - block * width
        for u in range(2):
            pick = (want == pk_c - u * width) & (pk_c // width == u)
            fa[u] = (mm(fw[...], flags(pick), NN) * 0.125).astype(BF16)
        wait_blocks(m, fsend, frecv, fs, fr)
        right_sq = []
        for h in range(2):
            sq = jnp.square(frecv[m, h].astype(F32))
            right_sq.append(mm(ones8, sq, NT, HI))

        def chunk(p, _):
            at = pl.ds(pl.multiple_of(p * QTR, QTR), QTR)
            left_sq = jnp.sum(jnp.square(fa[0, at, :].astype(F32)), axis=1, keepdims=True) * 4.0
            for h in range(2):
                for u in range(2):
                    cross = mm(fa[u, at, :], frecv[m, h], NT)
                    dist = left_sq + right_sq[h][u : u + 1, :]
                    col = h * HALF + u * QTR
                    q[m, at, col : col + QTR] = jnp.exp(cross - dist).astype(BF16)
            return 0

        lax.fori_loop(0, 4, chunk, 0)
        return 0

    lax.fori_loop(0, per, make_tile, 0)

    rh_r, rh_c = rows_cols((2 * width, lanes))
    ba_r, ba_c = rows_cols((width, lanes))

    def back_copy(it, m):
        return pltpu.make_async_remote_copy(
            src_ref=bsend.at[it, m], dst_ref=brecv.at[it, m],
            send_sem=bs.at[it, m], recv_sem=br.at[it, m],
            device_id={"blk": lax.rem(me - 2 * m - r + peers, peers), "rep": r},
            device_id_type=MESH,
        )

    for it in range(ITERS):
        last = it == ITERS - 1
        fill_own(lambda idx: yw[it, idx, :], yrecv.at[it])
        z[...] = jnp.zeros((BS, lanes), F32)

        def product(m, _):
            d = 2 * m + r
            back_block = own(d, True)
            y_t = mm(flags(ba_c == ba_r + back_block * width), yw[it], NT).astype(BF16)
            bsend[it, m] = mm(y_t, q[m], NN).astype(BF16)

            @pl.when(d != 0)
            def _():
                back_copy(it, m).start()

            @pl.when(d == 0)
            def _():
                brecv[it, m] = bsend[it, m]

            block = own(d, False)
            wait_blocks(m, ysend.at[it], yrecv.at[it], ys.at[it], yr.at[it])
            for h in range(2):
                for u in range(2):
                    place = flags((rh_r - u * width == rh_c - block * width) & (rh_r // width == u))
                    at = h * HALF + u * QTR
                    rhs[at : at + QTR, :] = mm(yrecv[it, m, h], place, NN).astype(BF16)

            def chunk(p, _):
                at = pl.ds(pl.multiple_of(p * QTR, QTR), QTR)
                z[at, :] += mm(q[m, at, :], rhs[...], NN)
                return 0

            lax.fori_loop(0, 4, chunk, 0)
            return 0

        lax.fori_loop(0, per, product, 0)

        def collect(m, _):
            d = 2 * m + r
            eb[m] = flags(ba_c == ba_r + asked(d) * width)

            @pl.when(d != 0)
            def _():
                back_copy(it, m).wait_recv()

            return 0

        lax.fori_loop(0, per, collect, 0)
        z[...] += mm(
            brecv[it].reshape(per * width, BS), eb[...].reshape(per * width, lanes), TN
        )

        twin = {"blk": me, "rep": 1 - r}
        if last:
            zs[0] = z[:, : lanes // 2]
            zs[1] = z[:, lanes // 2 :]
            swap = pltpu.make_async_remote_copy(
                src_ref=zs.at[1 - r], dst_ref=zx2, send_sem=zsem_s.at[it],
                recv_sem=zsem_r.at[it], device_id=twin, device_id_type=MESH,
            )
        else:
            swap = pltpu.make_async_remote_copy(
                src_ref=z.at[pl.ds(pl.multiple_of((1 - r) * HALF, HALF), HALF), :],
                dst_ref=zx1, send_sem=zsem_s.at[it],
                recv_sem=zsem_r.at[it], device_id=twin, device_id_type=MESH,
            )
        swap.start()
        swap.wait()
        if last:
            first = jnp.where(r == 0, 1.0, 0.0)
            mine_scale = scale[:, : lanes // 2] * first + scale[:, lanes // 2 :] * (1.0 - first)
            w = (zs[r] + zx2[...]) * mine_scale
        else:
            rows = pl.ds(pl.multiple_of(r * HALF, HALF), HALF)
            mine_scale = scale[rows, :]
            w = (z[rows, :] + zx1[...]) * mine_scale
        wl = w.shape[1]

        gg = mm(w, w, TN, HI)
        g_r, g_c = rows_cols((wl, wl))
        gg = jnp.where(g_r // width == g_c // width, gg, 0.0)
        a_r, a_c = rows_cols((width, wl))
        fold = flags(a_c % width == a_r, F32)
        b_r, b_c = rows_cols((2 * width, wl))
        fold_wide = flags(b_c % width == b_r, F32)
        gx[it, k] = mm(mm(fold, gg, NN, HI), fold_wide, NT, HI)

        def gram_copy(t, src):
            return pltpu.make_async_remote_copy(
                src_ref=gx.at[it, src], dst_ref=gx.at[it, src],
                send_sem=gs.at[it, t], recv_sem=gr.at[it, src],
                device_id=dev(lax.rem(k + t, devs)), device_id_type=MESH,
            )

        def gram_send(t, _):
            gram_copy(t, k).start()
            return 0

        def gram_wait(t, _):
            gram_copy(t, lax.rem(k + t, devs)).wait_recv()
            return 0

        def gram_done(t, _):
            gram_copy(t, k).wait_send()
            return 0

        lax.fori_loop(1, devs, gram_send, 0)
        lax.fori_loop(1, devs, gram_wait, 0)
        gram = gx[it, 0]
        for t in range(1, devs):
            gram = gram + gx[it, t]
        chol[...] = cholesky_and_inverse(gram * (1.0 / total_rows), width)

        c_r, c_c = rows_cols((wl, 2 * width))
        inv_t = mm(flags(c_c == width + c_r % width, F32), chol[...], NT, HI)
        t_r, t_c = rows_cols((width, wl))
        tiled = mm(inv_t, flags(t_c % width == t_r, F32), NN, HI)
        v = mm(w, jnp.where(g_r // width == g_c // width, tiled, 0.0), NN, HI)
        if last:
            for b in range(blocks // 2):
                p_r, p_c = rows_cols((wl, width))
                out[b * BS : (b + 1) * BS, :] = v[:, b * width : (b + 1) * width]
            l_r, l_c = rows_cols((width, 2 * width))
            factor[...] = mm(flags(l_r == l_c, F32), chol[...], NT, HI)
        else:
            yw[it + 1, rows, :] = (v * mine_scale).astype(BF16)
            give = pltpu.make_async_remote_copy(
                src_ref=yw.at[it + 1, rows, :], dst_ref=yw.at[it + 1, rows, :],
                send_sem=yos, recv_sem=yor, device_id=twin, device_id_type=MESH,
            )
            give.start()
            nxt = it + 1
            send_blocks(
                lambda idx: yw[nxt, idx, :], nxt,
                ysend.at[nxt], yrecv.at[nxt], ys.at[nxt], yr.at[nxt],
            )
            other = pl.ds(pl.multiple_of((1 - r) * HALF, HALF), HALF)
            give.wait_send()
            pltpu.make_async_remote_copy(
                src_ref=yw.at[it + 1, other, :], dst_ref=yw.at[it + 1, other, :],
                send_sem=yos, recv_sem=yor, device_id=twin, device_id_type=MESH,
            ).wait_recv()
        lax.fori_loop(1, devs, gram_done, 0)

    def blocks_done(d, _):
        block_copy(fsend, frecv, fs, fr, d, r).wait_send()
        for it in range(ITERS):
            block_copy(ysend.at[it], yrecv.at[it], ys.at[it], yr.at[it], d, r).wait_send()
        return 0

    lax.fori_loop(1, peers, blocks_done, 0)

    def info_done(t, _):
        info_copy(t, k).wait_send()
        return 0

    lax.fori_loop(1, devs, info_done, 0)

    def back_done(m, _):
        @pl.when(2 * m + r != 0)
        def _():
            for it in range(ITERS):
                back_copy(it, m).wait_send()

        return 0

    lax.fori_loop(0, per, back_done, 0)


def per_device(frames, degree, start, block_slot, pair_list, pair_count):
    peers = lax.axis_size("blk")
    local_rows, width = start.shape
    blocks = local_rows // BS
    slots = pair_list.shape[2]
    per = peers // 2
    devs = 2 * peers
    lanes = blocks * width
    dma = pltpu.SemaphoreType.DMA
    vmem = pl.BlockSpec(memory_space=pltpu.VMEM)
    smem = pl.BlockSpec(memory_space=pltpu.SMEM)
    scratch = [
        pltpu.VMEM((devs, 1, 128), jnp.int32),
        pltpu.SMEM((devs, 1, 128), jnp.int32),
        pltpu.VMEM((BS, lanes), BF16),
        pltpu.VMEM((ITERS, BS, lanes), BF16),
        pltpu.VMEM((BS, lanes), F32),
        pltpu.VMEM((peers, QTR, 2 * width), BF16),
        pltpu.VMEM((per, 2, QTR, 2 * width), BF16),
        pltpu.VMEM((ITERS, peers, QTR, 2 * width), BF16),
        pltpu.VMEM((ITERS, per, 2, QTR, 2 * width), BF16),
        pltpu.VMEM((2, BS, 2 * width), BF16),
        pltpu.VMEM((per, BS, BS), BF16),
        pltpu.VMEM((BS, lanes), BF16),
        pltpu.VMEM((BS, lanes), F32),
        pltpu.VMEM((2, BS, lanes // 2), F32),
        pltpu.VMEM((ITERS, per, width, BS), BF16),
        pltpu.VMEM((ITERS, per, width, BS), BF16),
        pltpu.VMEM((per, width, lanes), BF16),
        pltpu.VMEM((HALF, lanes), F32),
        pltpu.VMEM((BS, lanes // 2), F32),
        pltpu.VMEM((ITERS, devs, width, 2 * width), F32),
        pltpu.VMEM((width, 2 * width), F32),
        dma((devs,)), dma((devs,)), dma,
        dma((peers,)), dma((per, 2)),
        dma((ITERS, peers)), dma((ITERS, per, 2)),
        dma((ITERS, per)), dma((ITERS, per)),
        dma((ITERS,)), dma((ITERS,)),
        dma((ITERS, devs)), dma((ITERS, devs)),
        dma, dma,
    ]
    return pl.pallas_call(
        functools.partial(kernel, peers, blocks, width, slots, local_rows * peers),
        out_shape=(
            jax.ShapeDtypeStruct((local_rows // 2, width), F32),
            jax.ShapeDtypeStruct((width, width), F32),
        ),
        in_specs=[vmem, vmem, vmem, smem, smem, smem],
        out_specs=(vmem, vmem),
        scratch_shapes=scratch,
        compiler_params=pltpu.CompilerParams(
            collective_id=0, has_side_effects=True, vmem_limit_bytes=56 * 1024 * 1024
        ),
    )(
        frames,
        degree.reshape(blocks, BS),
        start,
        block_slot,
        pair_list.reshape(-1),
        pair_count.reshape(-1),
    )


def solution(mesh):
    placed = (
        P(("groups", "blk"), None),
        P(("groups", "blk")),
        P(("groups", "blk"), None),
        P("groups"),
        P(("groups", "blk"), "rep", None, None),
        P(("groups", "blk"), "rep"),
    )
    return jax.shard_map(
        per_device,
        mesh=mesh,
        in_specs=placed,
        out_specs=(P(("groups", "blk", "rep"), None), P("groups", None)),
        check_vma=False,
    )
```

```python
import functools

import jax
import jax.numpy as jnp
from jax import lax
from jax.experimental import pallas as pl
from jax.experimental.pallas import tpu as pltpu
from jax.sharding import PartitionSpec as P

BS = 1024
ITERS = 2
HALF = BS // 2
CHUNK = BS // 4
MESH = pl.DeviceIdType.MESH
F32 = jnp.float32
BF16 = jnp.bfloat16
HI = lax.Precision.HIGHEST
NN = ((1,), (0,))
NT = ((1,), (1,))
TN = ((0,), (0,))


def mm(a, b, dims, precision=None):
    return lax.dot_general(
        a, b, (dims, ((), ())), precision=precision, preferred_element_type=F32
    )


def rows_cols(shape):
    return (
        lax.broadcasted_iota(jnp.int32, shape, 0),
        lax.broadcasted_iota(jnp.int32, shape, 1),
    )


def flags(cond, dtype=BF16):
    return jnp.where(cond, 1.0, 0.0).astype(dtype)


def cholesky_and_inverse(gram, n):
    rows, cols = rows_cols((n, 2 * n))
    a = jnp.where(cols < n, gram, flags(cols == rows + n, F32))
    row_id = lax.broadcasted_iota(jnp.int32, (n, 1), 0)
    for j in range(n - 1):
        col = jnp.sum(jnp.where(cols == j, a, 0.0), axis=1, keepdims=True)
        mult = jnp.where(row_id > j, col, 0.0) / col[j : j + 1, :]
        a = a - mult * a[j : j + 1, :]
    diag = jnp.sum(jnp.where(cols == rows, a, 0.0), axis=1, keepdims=True)
    return a * lax.rsqrt(diag)


def kernel(
    peers, blocks, width, slots, total_rows,
    frames, degree, start, block_slot, pairs, count,
    out, factor,
    info, table, ft, fn, yt, scale, fsend, frecv, ysend, yrecv, q, ypl, zt, zx,
    bsend, brecv, eb, gx, chol,
    info_s, info_r, table_s, fs, fr, ys, yr, bs, br, zsem_s, zsem_r, gs, gr,
):
    me = lax.axis_index("blk")
    r = lax.axis_index("rep")
    k = 2 * me + r
    devs = 2 * peers
    per = peers // 2
    half_w = width // 2
    twin = {"blk": me, "rep": 1 - r}

    def dev(kk):
        return {"blk": kk // 2, "rep": lax.rem(kk, 2)}

    barrier = pltpu.get_barrier_semaphore()

    def greet(t, _):
        pl.semaphore_signal(
            barrier, inc=1, device_id=dev(lax.rem(k + t, devs)), device_id_type=MESH
        )
        return 0

    lax.fori_loop(1, devs, greet, 0)

    lane = lax.broadcasted_iota(jnp.int32, (1, 128), 1)
    mine = jnp.zeros((1, 128), jnp.int32)
    live_count = count[0]
    for s in range(slots):
        row = block_slot[pairs[2 * s]]
        col = block_slot[pairs[2 * s + 1]]
        peer = lax.div(col, blocks)
        alive = jnp.where(s < live_count, 1, 0)
        mine = jnp.where(lane == peer, (col - peer * blocks + 1) * alive, mine)
        mine = jnp.where(lane == 32 + peer, (row - me * blocks + 1) * alive, mine)
        mine = jnp.where(lane == 64 + peer, jnp.where(row != col, 1, 0) * alive, mine)
    info[k] = mine

    for b in range(blocks):
        at = slice(b * BS, (b + 1) * BS)
        ft[b] = frames[:, at]

    pl.semaphore_wait(barrier, devs - 1)

    def info_copy(t, src):
        return pltpu.make_async_remote_copy(
            src_ref=info.at[src], dst_ref=info.at[src],
            send_sem=info_s.at[t], recv_sem=info_r.at[src],
            device_id=dev(lax.rem(k + t, devs)), device_id_type=MESH,
        )

    def info_send(t, _):
        info_copy(t, k).start()
        return 0

    lax.fori_loop(1, devs, info_send, 0)

    for b in range(blocks):
        at = slice(b * BS, (b + 1) * BS)
        s_row = lax.rsqrt(degree[:, at])
        scale[b] = s_row
        yt[0, b] = (start[:, at] * s_row).astype(BF16)
        e_r, e_c = rows_cols((width, width))
        fn[b] = (mm(ft[b], flags(e_r == e_c), TN) * 0.125).astype(BF16)

    def info_wait(t, _):
        info_copy(t, lax.rem(k + t, devs)).wait_recv()
        return 0

    lax.fori_loop(1, devs, info_wait, 0)
    to_table = pltpu.make_async_copy(info, table, table_s)
    to_table.start()
    to_table.wait()

    def asked(d):
        owner = lax.rem(me + d, peers)
        return table[2 * owner, 0, me] + table[2 * owner + 1, 0, me] - 1

    def own(d):
        peer = 32 + lax.rem(me - d + peers, peers)
        return table[2 * me, 0, peer] + table[2 * me + 1, 0, peer] - 1

    def differ(d):
        peer = 64 + lax.rem(me - d + peers, peers)
        return table[2 * me, 0, peer] + table[2 * me + 1, 0, peer]

    def lanes_of(half):
        return pl.ds(pl.multiple_of(half * HALF, HALF), HALF)

    def block_copy(send, recv, ssem, rsem, d, half):
        return pltpu.make_async_remote_copy(
            src_ref=send.at[d], dst_ref=recv.at[d // 2, half],
            send_sem=ssem.at[d], recv_sem=rsem.at[d // 2, half],
            device_id={"blk": lax.rem(me + d, peers), "rep": lax.rem(d, 2)},
            device_id_type=MESH,
        )

    def send_blocks(source, send, recv, ssem, rsem):
        def one(d, _):
            send[d] = source[jnp.maximum(asked(d), 0), :, lanes_of(r)]
            block_copy(send, recv, ssem, rsem, d, r).start()
            return 0

        lax.fori_loop(1, peers, one, 0)

    def fill_own(source, recv):
        @pl.when(r == 0)
        def _():
            block = jnp.maximum(asked(0), 0)
            for half in range(2):
                recv[0, half] = source[block, :, half * HALF : (half + 1) * HALF]

    def wait_blocks(m, send, recv, ssem, rsem):
        @pl.when(2 * m + r != 0)
        def _():
            for half in range(2):
                pltpu.make_async_remote_copy(
                    src_ref=send.at[0], dst_ref=recv.at[m, half],
                    send_sem=ssem.at[0], recv_sem=rsem.at[m, half],
                    device_id=twin, device_id_type=MESH,
                ).wait_recv()

    send_blocks(ft, fsend, frecv, fs, fr)
    send_blocks(yt.at[0], ysend.at[0], yrecv.at[0], ys.at[0], yr.at[0])
    fill_own(ft, frecv)

    def back_copy(it, m):
        return pltpu.make_async_remote_copy(
            src_ref=bsend.at[it, m], dst_ref=brecv.at[it, m],
            send_sem=bs.at[it, m], recv_sem=br.at[it, m],
            device_id={"blk": lax.rem(me - 2 * m - r + peers, peers), "rep": r},
            device_id_type=MESH,
        )

    def send_back(it, m):
        d = 2 * m + r
        keep = jnp.where(differ(d) > 0, 1.0, 0.0)
        y_a = (yt[it, jnp.maximum(own(d), 0)].astype(F32) * keep).astype(BF16)
        bsend[it, m] = mm(y_a, q[m], NN).astype(BF16)

        @pl.when(d != 0)
        def _():
            back_copy(it, m).start()

        @pl.when(d == 0)
        def _():
            brecv[it, m] = bsend[it, m]

    def make_tile(m, _):
        block = jnp.maximum(own(2 * m + r), 0)
        wait_blocks(m, fsend, frecv, fs, fr)
        right_sq = [
            jnp.sum(jnp.square(frecv[m, h].astype(F32)), axis=0, keepdims=True) * (1.0 / 16.0)
            for h in range(2)
        ]

        def chunk(p, _):
            at = pl.ds(pl.multiple_of(p * CHUNK, CHUNK), CHUNK)
            left = fn[block, at, :]
            left_sq = jnp.sum(jnp.square(left.astype(F32)), axis=1, keepdims=True) * 4.0
            for h in range(2):
                cross = mm(left, frecv[m, h], NN)
                dist = left_sq + right_sq[h]
                q[m, at, h * HALF : (h + 1) * HALF] = jnp.exp(cross - dist).astype(BF16)
            return 0

        lax.fori_loop(0, BS // CHUNK, chunk, 0)
        send_back(0, m)
        return 0

    lax.fori_loop(0, per, make_tile, 0)

    pl_r, pl_c = rows_cols((blocks * width, width))

    for it in range(ITERS):
        last = it == ITERS - 1
        fill_own(yt.at[it], yrecv.at[it])
        if it > 0:

            def back(m, _):
                send_back(it, m)
                return 0

            lax.fori_loop(0, per, back, 0)
        zt[...] = jnp.zeros_like(zt)

        def product(m, _):
            wait_blocks(m, ysend.at[it], yrecv.at[it], ys.at[it], yr.at[it])
            place = flags(pl_r == pl_c + own(2 * m + r) * width)
            for h in range(2):
                ypl[:, h * HALF : (h + 1) * HALF] = mm(place, yrecv[it, m, h], NN).astype(BF16)

            def chunk(p, _):
                at = pl.ds(pl.multiple_of(p * CHUNK, CHUNK), CHUNK)
                zt[:, at] += mm(ypl[...], q[m, at, :], NT)
                return 0

            lax.fori_loop(0, BS // CHUNK, chunk, 0)
            return 0

        lax.fori_loop(0, per, product, 0)

        def collect(m, _):
            d = 2 * m + r
            eb[m] = flags((pl_r == pl_c + asked(d) * width) & (asked(d) >= 0))

            @pl.when(d != 0)
            def _():
                back_copy(it, m).wait_recv()

            return 0

        lax.fori_loop(0, per, collect, 0)
        total = zt[...]
        for m in range(per):
            total = total + mm(eb[m], brecv[it, m], NN)
        zt[...] = total

        swap = pltpu.make_async_remote_copy(
            src_ref=zt, dst_ref=zx.at[it], send_sem=zsem_s.at[it],
            recv_sem=zsem_r.at[it], device_id=twin, device_id_type=MESH,
        )
        swap.start()
        swap.wait()
        for b in range(blocks):
            at = slice(b * width, (b + 1) * width)
            zt[at, :] = (zt[at, :] + zx[it, at, :]) * scale[b]

        gram = jnp.zeros((2 * width, 2 * width), F32)
        for b in range(0, blocks, 2):
            w_t = zt[b * width : (b + 2) * width, :]
            gram = gram + mm(w_t, w_t, NT, HI)
        gram = gram[:width] + pltpu.roll(gram[width:], width, 1)
        low = rows_cols((half_w, 2 * width))[1] < width
        gx[it, me] = jnp.where(low, gram[:half_w], pltpu.roll(gram[half_w:], width, 1))

        def gram_copy(t, src):
            return pltpu.make_async_remote_copy(
                src_ref=gx.at[it, src], dst_ref=gx.at[it, src],
                send_sem=gs.at[it, t], recv_sem=gr.at[it, src],
                device_id={"blk": lax.rem(me + t, peers), "rep": r}, device_id_type=MESH,
            )

        def gram_send(t, _):
            gram_copy(t, me).start()
            return 0

        def gram_wait(t, _):
            gram_copy(t, lax.rem(me + t, peers)).wait_recv()
            return 0

        def gram_done(t, _):
            gram_copy(t, me).wait_send()
            return 0

        lax.fori_loop(1, peers, gram_send, 0)
        lax.fori_loop(1, peers, gram_wait, 0)
        gram = gx[it, 0]
        for t in range(1, peers):
            gram = gram + gx[it, t]
        gram = jnp.concatenate([gram, pltpu.roll(gram, width, 1)], axis=0)
        result = cholesky_and_inverse(gram * (1.0 / total_rows), width)

        inverse = pltpu.roll(result, width, 1)[:, :width]
        if last:
            for b in range(blocks // 2):
                at = pl.ds(pl.multiple_of((r * (blocks // 2) + b) * width, width), width)
                out[:, b * BS : (b + 1) * BS] = mm(inverse, zt[at, :], NN, HI)
            chol[...] = result
            l_r, l_c = rows_cols((width, 2 * width))
            factor[...] = mm(flags(l_r == l_c, F32), chol[...], NT, HI)
        else:
            for b in range(blocks):
                v_t = mm(inverse, zt[b * width : (b + 1) * width, :], NN, HI)
                yt[it + 1, b] = (v_t * scale[b]).astype(BF16)
            nxt = it + 1
            send_blocks(yt.at[nxt], ysend.at[nxt], yrecv.at[nxt], ys.at[nxt], yr.at[nxt])
        lax.fori_loop(1, peers, gram_done, 0)

    def blocks_done(d, _):
        block_copy(fsend, frecv, fs, fr, d, r).wait_send()
        for it in range(ITERS):
            block_copy(ysend.at[it], yrecv.at[it], ys.at[it], yr.at[it], d, r).wait_send()
        return 0

    lax.fori_loop(1, peers, blocks_done, 0)

    def info_done(t, _):
        info_copy(t, k).wait_send()
        return 0

    lax.fori_loop(1, devs, info_done, 0)

    def back_done(m, _):
        @pl.when(2 * m + r != 0)
        def _():
            for it in range(ITERS):
                back_copy(it, m).wait_send()

        return 0

    lax.fori_loop(0, per, back_done, 0)


def per_device(frames, degree, start, block_slot, pair_list, pair_count):
    peers = lax.axis_size("blk")
    local_rows, width = start.shape
    blocks = local_rows // BS
    slots = pair_list.shape[2]
    per = peers // 2
    devs = 2 * peers
    dma = pltpu.SemaphoreType.DMA
    vmem = pl.BlockSpec(memory_space=pltpu.VMEM)
    smem = pl.BlockSpec(memory_space=pltpu.SMEM)
    scratch = [
        pltpu.VMEM((devs, 1, 128), jnp.int32),
        pltpu.SMEM((devs, 1, 128), jnp.int32),
        pltpu.VMEM((blocks, width, BS), BF16),
        pltpu.VMEM((blocks, BS, width), BF16),
        pltpu.VMEM((ITERS, blocks, width, BS), BF16),
        pltpu.VMEM((blocks, 1, BS), F32),
        pltpu.VMEM((peers, width, HALF), BF16),
        pltpu.VMEM((per, 2, width, HALF), BF16),
        pltpu.VMEM((ITERS, peers, width, HALF), BF16),
        pltpu.VMEM((ITERS, per, 2, width, HALF), BF16),
        pltpu.VMEM((per, BS, BS), BF16),
        pltpu.VMEM((blocks * width, BS), BF16),
        pltpu.VMEM((blocks * width, BS), F32),
        pltpu.VMEM((ITERS, blocks * width, BS), F32),
        pltpu.VMEM((ITERS, per, width, BS), BF16),
        pltpu.VMEM((ITERS, per, width, BS), BF16),
        pltpu.VMEM((per, blocks * width, width), BF16),
        pltpu.VMEM((ITERS, peers, width // 2, 2 * width), F32),
        pltpu.VMEM((width, 2 * width), F32),
        dma((devs,)), dma((devs,)), dma,
        dma((peers,)), dma((per, 2)),
        dma((ITERS, peers)), dma((ITERS, per, 2)),
        dma((ITERS, per)), dma((ITERS, per)),
        dma((ITERS,)), dma((ITERS,)),
        dma((ITERS, peers)), dma((ITERS, peers)),
    ]
    out_t, factor = pl.pallas_call(
        functools.partial(kernel, peers, blocks, width, slots, local_rows * peers),
        out_shape=(
            jax.ShapeDtypeStruct((width, local_rows // 2), F32),
            jax.ShapeDtypeStruct((width, width), F32),
        ),
        in_specs=[vmem, vmem, vmem, smem, smem, smem],
        out_specs=(vmem, vmem),
        scratch_shapes=scratch,
        compiler_params=pltpu.CompilerParams(
            collective_id=0, has_side_effects=True, vmem_limit_bytes=56 * 1024 * 1024
        ),
    )(
        frames.T,
        degree.reshape(1, local_rows),
        start.T,
        block_slot,
        pair_list.reshape(-1),
        pair_count.reshape(-1),
    )
    return out_t.T, factor


def solution(mesh):
    placed = (
        P(("groups", "blk"), None),
        P(("groups", "blk")),
        P(("groups", "blk"), None),
        P("groups"),
        P(("groups", "blk"), "rep", None, None),
        P(("groups", "blk"), "rep"),
    )
    return jax.shard_map(
        per_device,
        mesh=mesh,
        in_specs=placed,
        out_specs=(P(("groups", "blk", "rep"), None), P("groups", None)),
        check_vma=False,
    )
```

```python
import functools

import jax
import jax.numpy as jnp
from jax import lax
from jax.experimental import pallas as pl
from jax.experimental.pallas import tpu as pltpu
from jax.sharding import PartitionSpec as P

BS = 1024
ITERS = 2
HALF = BS // 2
CHUNK = BS // 4
MESH = pl.DeviceIdType.MESH
F32 = jnp.float32
BF16 = jnp.bfloat16
HI = lax.Precision.HIGHEST
NN = ((1,), (0,))
NT = ((1,), (1,))
TN = ((0,), (0,))


def mm(a, b, dims, precision=None):
    return lax.dot_general(
        a, b, (dims, ((), ())), precision=precision, preferred_element_type=F32
    )


def rows_cols(shape):
    return (
        lax.broadcasted_iota(jnp.int32, shape, 0),
        lax.broadcasted_iota(jnp.int32, shape, 1),
    )


def flags(cond, dtype=BF16):
    return jnp.where(cond, 1.0, 0.0).astype(dtype)


def cholesky_and_inverse(gram, n):
    rows, cols = rows_cols((n, 2 * n))
    a = jnp.where(cols < n, gram, flags(cols == rows + n, F32))
    row_id = lax.broadcasted_iota(jnp.int32, (n, 1), 0)
    for j in range(n - 1):
        col = jnp.sum(jnp.where(cols == j, a, 0.0), axis=1, keepdims=True)
        pivot = a[j : j + 1, :]
        inv = 1.0 / jnp.sum(jnp.where(cols[:1] == j, pivot, 0.0), axis=1, keepdims=True)
        a = a - jnp.where(row_id > j, col, 0.0) * (pivot * inv)
    diag = jnp.sum(jnp.where(cols == rows, a, 0.0), axis=1, keepdims=True)
    return a * lax.rsqrt(diag)


def kernel(
    peers, blocks, width, slots, total_rows,
    frames, degree, start, block_slot, pairs, count,
    out, factor,
    info, table, ft, fn, yt, scale, fsend, frecv, ysend, yrecv, q, ypl, zt, zx,
    bsend, brecv, eb, gx, chol,
    info_s, info_r, table_s, fs, fr, ys, yr, bs, br, zsem_s, zsem_r, gs, gr,
):
    me = lax.axis_index("blk")
    r = lax.axis_index("rep")
    k = 2 * me + r
    devs = 2 * peers
    per = peers // 2
    half_w = width // 2
    twin = {"blk": me, "rep": 1 - r}

    def dev(kk):
        return {"blk": kk // 2, "rep": lax.rem(kk, 2)}

    barrier = pltpu.get_barrier_semaphore()

    def greet(t, _):
        pl.semaphore_signal(
            barrier, inc=1, device_id=dev(lax.rem(k + t, devs)), device_id_type=MESH
        )
        return 0

    lax.fori_loop(1, devs, greet, 0)

    lane = lax.broadcasted_iota(jnp.int32, (1, 128), 1)
    mine = jnp.zeros((1, 128), jnp.int32)
    live_count = count[0]
    for s in range(slots):
        row = block_slot[pairs[2 * s]]
        col = block_slot[pairs[2 * s + 1]]
        peer = lax.div(col, blocks)
        alive = jnp.where(s < live_count, 1, 0)
        mine = jnp.where(lane == peer, (col - peer * blocks + 1) * alive, mine)
        mine = jnp.where(lane == 32 + peer, (row - me * blocks + 1) * alive, mine)
        mine = jnp.where(lane == 64 + peer, jnp.where(row != col, 1, 0) * alive, mine)
    info[k] = mine

    for b in range(blocks):
        at = slice(b * BS, (b + 1) * BS)
        ft[b] = frames[:, at]

    pl.semaphore_wait(barrier, devs - 1)

    def info_copy(t, src):
        return pltpu.make_async_remote_copy(
            src_ref=info.at[src], dst_ref=info.at[src],
            send_sem=info_s.at[t], recv_sem=info_r.at[src],
            device_id=dev(lax.rem(k + t, devs)), device_id_type=MESH,
        )

    def info_send(t, _):
        info_copy(t, k).start()
        return 0

    lax.fori_loop(1, devs, info_send, 0)

    for b in range(blocks):
        at = slice(b * BS, (b + 1) * BS)
        s_row = lax.rsqrt(degree[:, at])
        scale[b] = s_row
        yt[0, b] = (start[:, at] * s_row).astype(BF16)
        e_r, e_c = rows_cols((width, width))
        fn[b] = (mm(ft[b], flags(e_r == e_c), TN) * 0.125).astype(BF16)

    def info_wait(t, _):
        info_copy(t, lax.rem(k + t, devs)).wait_recv()
        return 0

    lax.fori_loop(1, devs, info_wait, 0)
    to_table = pltpu.make_async_copy(info, table, table_s)
    to_table.start()
    to_table.wait()

    def asked(d):
        owner = lax.rem(me + d, peers)
        return table[2 * owner, 0, me] + table[2 * owner + 1, 0, me] - 1

    def own(d):
        peer = 32 + lax.rem(me - d + peers, peers)
        return table[2 * me, 0, peer] + table[2 * me + 1, 0, peer] - 1

    def differ(d):
        peer = 64 + lax.rem(me - d + peers, peers)
        return table[2 * me, 0, peer] + table[2 * me + 1, 0, peer]

    def lanes_of(half):
        return pl.ds(pl.multiple_of(half * HALF, HALF), HALF)

    def block_copy(send, recv, ssem, rsem, d, half):
        return pltpu.make_async_remote_copy(
            src_ref=send.at[d], dst_ref=recv.at[d // 2, half],
            send_sem=ssem.at[d], recv_sem=rsem.at[d // 2, half],
            device_id={"blk": lax.rem(me + d, peers), "rep": lax.rem(d, 2)},
            device_id_type=MESH,
        )

    def send_blocks(source, send, recv, ssem, rsem):
        def one(d, _):
            send[d] = source[jnp.maximum(asked(d), 0), :, lanes_of(r)]
            block_copy(send, recv, ssem, rsem, d, r).start()
            return 0

        lax.fori_loop(1, peers, one, 0)

    def fill_own(source, recv):
        @pl.when(r == 0)
        def _():
            block = jnp.maximum(asked(0), 0)
            for half in range(2):
                recv[0, half] = source[block, :, half * HALF : (half + 1) * HALF]

    def wait_blocks(m, send, recv, ssem, rsem):
        @pl.when(2 * m + r != 0)
        def _():
            for half in range(2):
                pltpu.make_async_remote_copy(
                    src_ref=send.at[0], dst_ref=recv.at[m, half],
                    send_sem=ssem.at[0], recv_sem=rsem.at[m, half],
                    device_id=twin, device_id_type=MESH,
                ).wait_recv()

    send_blocks(ft, fsend, frecv, fs, fr)
    send_blocks(yt.at[0], ysend.at[0], yrecv.at[0], ys.at[0], yr.at[0])
    fill_own(ft, frecv)

    def back_copy(it, m):
        return pltpu.make_async_remote_copy(
            src_ref=bsend.at[it, m], dst_ref=brecv.at[it, m],
            send_sem=bs.at[it, m], recv_sem=br.at[it, m],
            device_id={"blk": lax.rem(me - 2 * m - r + peers, peers), "rep": r},
            device_id_type=MESH,
        )

    def send_back(it, m):
        d = 2 * m + r
        keep = jnp.where(differ(d) > 0, 1.0, 0.0)
        y_a = (yt[it, jnp.maximum(own(d), 0)].astype(F32) * keep).astype(BF16)
        bsend[it, m] = mm(y_a, q[m], NN).astype(BF16)

        @pl.when(d != 0)
        def _():
            back_copy(it, m).start()

        @pl.when(d == 0)
        def _():
            brecv[it, m] = bsend[it, m]

    def make_tile(m, _):
        block = jnp.maximum(own(2 * m + r), 0)
        wait_blocks(m, fsend, frecv, fs, fr)
        right_sq = [
            jnp.sum(jnp.square(frecv[m, h].astype(F32)), axis=0, keepdims=True) * (1.0 / 16.0)
            for h in range(2)
        ]

        def chunk(p, _):
            at = pl.ds(pl.multiple_of(p * CHUNK, CHUNK), CHUNK)
            left = fn[block, at, :]
            left_sq = jnp.sum(jnp.square(left.astype(F32)), axis=1, keepdims=True) * 4.0
            for h in range(2):
                cross = mm(left, frecv[m, h], NN)
                dist = left_sq + right_sq[h]
                q[m, at, h * HALF : (h + 1) * HALF] = jnp.exp(cross - dist).astype(BF16)
            return 0

        lax.fori_loop(0, BS // CHUNK, chunk, 0)
        send_back(0, m)
        return 0

    lax.fori_loop(0, per, make_tile, 0)

    pl_r, pl_c = rows_cols((blocks * width, width))

    for it in range(ITERS):
        last = it == ITERS - 1
        fill_own(yt.at[it], yrecv.at[it])
        if it > 0:

            def back(m, _):
                send_back(it, m)
                return 0

            lax.fori_loop(0, per, back, 0)
        zt[...] = jnp.zeros_like(zt)

        def product(m, _):
            wait_blocks(m, ysend.at[it], yrecv.at[it], ys.at[it], yr.at[it])
            place = flags(pl_r == pl_c + own(2 * m + r) * width)
            for h in range(2):
                ypl[:, h * HALF : (h + 1) * HALF] = mm(place, yrecv[it, m, h], NN).astype(BF16)

            def chunk(p, _):
                at = pl.ds(pl.multiple_of(p * CHUNK, CHUNK), CHUNK)
                zt[:, at] += mm(ypl[...], q[m, at, :], NT)
                return 0

            lax.fori_loop(0, BS // CHUNK, chunk, 0)
            return 0

        lax.fori_loop(0, per, product, 0)

        def collect(m, _):
            d = 2 * m + r
            eb[m] = flags((pl_r == pl_c + asked(d) * width) & (asked(d) >= 0))

            @pl.when(d != 0)
            def _():
                back_copy(it, m).wait_recv()

            return 0

        lax.fori_loop(0, per, collect, 0)
        total = zt[...]
        for m in range(per):
            total = total + mm(eb[m], brecv[it, m], NN)
        zt[...] = total

        swap = pltpu.make_async_remote_copy(
            src_ref=zt, dst_ref=zx.at[it], send_sem=zsem_s.at[it],
            recv_sem=zsem_r.at[it], device_id=twin, device_id_type=MESH,
        )
        swap.start()
        swap.wait()
        for b in range(blocks):
            at = slice(b * width, (b + 1) * width)
            zt[at, :] = (zt[at, :] + zx[it, at, :]) * scale[b]

        gram = jnp.zeros((2 * width, 2 * width), F32)
        for b in range(0, blocks, 2):
            w_t = zt[b * width : (b + 2) * width, :]
            gram = gram + mm(w_t, w_t, NT, HI)
        gram = gram[:width] + pltpu.roll(gram[width:], width, 1)
        low = rows_cols((half_w, 2 * width))[1] < width
        gx[it, me] = jnp.where(low, gram[:half_w], pltpu.roll(gram[half_w:], width, 1))

        def gram_copy(t, src):
            return pltpu.make_async_remote_copy(
                src_ref=gx.at[it, src], dst_ref=gx.at[it, src],
                send_sem=gs.at[it, t], recv_sem=gr.at[it, src],
                device_id={"blk": lax.rem(me + t, peers), "rep": r}, device_id_type=MESH,
            )

        def gram_send(t, _):
            gram_copy(t, me).start()
            return 0

        def gram_wait(t, _):
            gram_copy(t, lax.rem(me + t, peers)).wait_recv()
            return 0

        def gram_done(t, _):
            gram_copy(t, me).wait_send()
            return 0

        lax.fori_loop(1, peers, gram_send, 0)
        lax.fori_loop(1, peers, gram_wait, 0)
        gram = gx[it, 0]
        for t in range(1, peers):
            gram = gram + gx[it, t]
        gram = jnp.concatenate([gram, pltpu.roll(gram, width, 1)], axis=0)
        result = cholesky_and_inverse(gram * (1.0 / total_rows), width)

        inverse = pltpu.roll(result, width, 1)[:, :width]
        if last:
            for b in range(blocks // 2):
                at = pl.ds(pl.multiple_of((r * (blocks // 2) + b) * width, width), width)
                out[:, b * BS : (b + 1) * BS] = mm(inverse, zt[at, :], NN, HI)
            chol[...] = result
            l_r, l_c = rows_cols((width, 2 * width))
            factor[...] = mm(flags(l_r == l_c, F32), chol[...], NT, HI)
        else:
            for b in range(blocks):
                v_t = mm(inverse, zt[b * width : (b + 1) * width, :], NN, HI)
                yt[it + 1, b] = (v_t * scale[b]).astype(BF16)
            nxt = it + 1
            send_blocks(yt.at[nxt], ysend.at[nxt], yrecv.at[nxt], ys.at[nxt], yr.at[nxt])
        lax.fori_loop(1, peers, gram_done, 0)

    def blocks_done(d, _):
        block_copy(fsend, frecv, fs, fr, d, r).wait_send()
        for it in range(ITERS):
            block_copy(ysend.at[it], yrecv.at[it], ys.at[it], yr.at[it], d, r).wait_send()
        return 0

    lax.fori_loop(1, peers, blocks_done, 0)

    def info_done(t, _):
        info_copy(t, k).wait_send()
        return 0

    lax.fori_loop(1, devs, info_done, 0)

    def back_done(m, _):
        @pl.when(2 * m + r != 0)
        def _():
            for it in range(ITERS):
                back_copy(it, m).wait_send()

        return 0

    lax.fori_loop(0, per, back_done, 0)


def per_device(frames, degree, start, block_slot, pair_list, pair_count):
    peers = lax.axis_size("blk")
    local_rows, width = start.shape
    blocks = local_rows // BS
    slots = pair_list.shape[2]
    per = peers // 2
    devs = 2 * peers
    dma = pltpu.SemaphoreType.DMA
    vmem = pl.BlockSpec(memory_space=pltpu.VMEM)
    smem = pl.BlockSpec(memory_space=pltpu.SMEM)
    scratch = [
        pltpu.VMEM((devs, 1, 128), jnp.int32),
        pltpu.SMEM((devs, 1, 128), jnp.int32),
        pltpu.VMEM((blocks, width, BS), BF16),
        pltpu.VMEM((blocks, BS, width), BF16),
        pltpu.VMEM((ITERS, blocks, width, BS), BF16),
        pltpu.VMEM((blocks, 1, BS), F32),
        pltpu.VMEM((peers, width, HALF), BF16),
        pltpu.VMEM((per, 2, width, HALF), BF16),
        pltpu.VMEM((ITERS, peers, width, HALF), BF16),
        pltpu.VMEM((ITERS, per, 2, width, HALF), BF16),
        pltpu.VMEM((per, BS, BS), BF16),
        pltpu.VMEM((blocks * width, BS), BF16),
        pltpu.VMEM((blocks * width, BS), F32),
        pltpu.VMEM((ITERS, blocks * width, BS), F32),
        pltpu.VMEM((ITERS, per, width, BS), BF16),
        pltpu.VMEM((ITERS, per, width, BS), BF16),
        pltpu.VMEM((per, blocks * width, width), BF16),
        pltpu.VMEM((ITERS, peers, width // 2, 2 * width), F32),
        pltpu.VMEM((width, 2 * width), F32),
        dma((devs,)), dma((devs,)), dma,
        dma((peers,)), dma((per, 2)),
        dma((ITERS, peers)), dma((ITERS, per, 2)),
        dma((ITERS, per)), dma((ITERS, per)),
        dma((ITERS,)), dma((ITERS,)),
        dma((ITERS, peers)), dma((ITERS, peers)),
    ]
    out_t, factor = pl.pallas_call(
        functools.partial(kernel, peers, blocks, width, slots, local_rows * peers),
        out_shape=(
            jax.ShapeDtypeStruct((width, local_rows // 2), F32),
            jax.ShapeDtypeStruct((width, width), F32),
        ),
        in_specs=[vmem, vmem, vmem, smem, smem, smem],
        out_specs=(vmem, vmem),
        scratch_shapes=scratch,
        compiler_params=pltpu.CompilerParams(
            collective_id=0, has_side_effects=True, vmem_limit_bytes=56 * 1024 * 1024
        ),
    )(
        frames.T,
        degree.reshape(1, local_rows),
        start.T,
        block_slot,
        pair_list.reshape(-1),
        pair_count.reshape(-1),
    )
    return out_t.T, factor


def solution(mesh):
    placed = (
        P(("groups", "blk"), None),
        P(("groups", "blk")),
        P(("groups", "blk"), None),
        P("groups"),
        P(("groups", "blk"), "rep", None, None),
        P(("groups", "blk"), "rep"),
    )
    return jax.shard_map(
        per_device,
        mesh=mesh,
        in_specs=placed,
        out_specs=(P(("groups", "blk", "rep"), None), P("groups", None)),
        check_vma=False,
    )
```

```python
import functools

import jax
import jax.numpy as jnp
from jax import lax
from jax.experimental import pallas as pl
from jax.experimental.pallas import tpu as pltpu
from jax.sharding import PartitionSpec as P

BS = 1024
ITERS = 2
HALF = BS // 2
CHUNK = BS // 4
MESH = pl.DeviceIdType.MESH
F32 = jnp.float32
BF16 = jnp.bfloat16
HI = lax.Precision.HIGHEST
NN = ((1,), (0,))
NT = ((1,), (1,))
TN = ((0,), (0,))


def mm(a, b, dims, precision=None):
    return lax.dot_general(
        a, b, (dims, ((), ())), precision=precision, preferred_element_type=F32
    )


def rows_cols(shape):
    return (
        lax.broadcasted_iota(jnp.int32, shape, 0),
        lax.broadcasted_iota(jnp.int32, shape, 1),
    )


def flags(cond, dtype=BF16):
    return jnp.where(cond, 1.0, 0.0).astype(dtype)


def cholesky_and_inverse(gram, n):
    rows, cols = rows_cols((n, 2 * n))
    a = jnp.where(cols < n, gram, flags(cols == rows + n, F32))
    row_id = lax.broadcasted_iota(jnp.int32, (n, 1), 0)
    for j in range(n - 1):
        col = jnp.sum(jnp.where(cols == j, a, 0.0), axis=1, keepdims=True)
        mult = jnp.where(row_id > j, col, 0.0) / col[j : j + 1, :]
        a = a - mult * a[j : j + 1, :]
    diag = jnp.sum(jnp.where(cols == rows, a, 0.0), axis=1, keepdims=True)
    return a * lax.rsqrt(diag)


def kernel(
    peers, blocks, width, slots, total_rows,
    frames, degree, start, block_slot, pairs, count,
    out, factor,
    info, table, ft, fn, yt, scale, fsend, frecv, ysend, yrecv, q, ypl, zt, zx,
    bsend, brecv, eb, gx, chol,
    info_s, info_r, table_s, fs, fr, ys, yr, bs, br, zsem_s, zsem_r, gs, gr,
):
    me = lax.axis_index("blk")
    r = lax.axis_index("rep")
    k = 2 * me + r
    devs = 2 * peers
    per = peers // 2
    half_w = width // 2
    twin = {"blk": me, "rep": 1 - r}

    def dev(kk):
        return {"blk": kk // 2, "rep": lax.rem(kk, 2)}

    barrier = pltpu.get_barrier_semaphore()

    def greet(t, _):
        pl.semaphore_signal(
            barrier, inc=1, device_id=dev(lax.rem(k + t, devs)), device_id_type=MESH
        )
        return 0

    lax.fori_loop(1, devs, greet, 0)

    lane = lax.broadcasted_iota(jnp.int32, (1, 128), 1)
    mine = jnp.zeros((1, 128), jnp.int32)
    live_count = count[0]
    for s in range(slots):
        row = block_slot[pairs[2 * s]]
        col = block_slot[pairs[2 * s + 1]]
        peer = lax.div(col, blocks)
        alive = jnp.where(s < live_count, 1, 0)
        mine = jnp.where(lane == peer, (col - peer * blocks + 1) * alive, mine)
        mine = jnp.where(lane == 32 + peer, (row - me * blocks + 1) * alive, mine)
        mine = jnp.where(lane == 64 + peer, jnp.where(row != col, 1, 0) * alive, mine)
    info[k] = mine

    for b in range(blocks):
        at = slice(b * BS, (b + 1) * BS)
        ft[b] = frames[:, at]

    pl.semaphore_wait(barrier, devs - 1)

    def info_copy(t, src):
        return pltpu.make_async_remote_copy(
            src_ref=info.at[src], dst_ref=info.at[src],
            send_sem=info_s.at[t], recv_sem=info_r.at[src],
            device_id=dev(lax.rem(k + t, devs)), device_id_type=MESH,
        )

    def info_send(t, _):
        info_copy(t, k).start()
        return 0

    lax.fori_loop(1, devs, info_send, 0)

    for b in range(blocks):
        at = slice(b * BS, (b + 1) * BS)
        s_row = lax.rsqrt(degree[:, at])
        scale[b] = s_row
        yt[0, b] = (start[:, at] * s_row).astype(BF16)
        e_r, e_c = rows_cols((width, width))
        fn[b] = (mm(ft[b], flags(e_r == e_c), TN) * 0.125).astype(BF16)

    def info_wait(t, _):
        info_copy(t, lax.rem(k + t, devs)).wait_recv()
        return 0

    lax.fori_loop(1, devs, info_wait, 0)
    to_table = pltpu.make_async_copy(info, table, table_s)
    to_table.start()
    to_table.wait()

    def asked(d):
        owner = lax.rem(me + d, peers)
        return table[2 * owner, 0, me] + table[2 * owner + 1, 0, me] - 1

    def own(d):
        peer = 32 + lax.rem(me - d + peers, peers)
        return table[2 * me, 0, peer] + table[2 * me + 1, 0, peer] - 1

    def differ(d):
        peer = 64 + lax.rem(me - d + peers, peers)
        return table[2 * me, 0, peer] + table[2 * me + 1, 0, peer]

    def lanes_of(half):
        return pl.ds(pl.multiple_of(half * HALF, HALF), HALF)

    def block_copy(send, recv, ssem, rsem, d, half):
        return pltpu.make_async_remote_copy(
            src_ref=send.at[d], dst_ref=recv.at[d // 2, half],
            send_sem=ssem.at[d], recv_sem=rsem.at[d // 2, half],
            device_id={"blk": lax.rem(me + d, peers), "rep": lax.rem(d, 2)},
            device_id_type=MESH,
        )

    def send_blocks(source, send, recv, ssem, rsem):
        def one(d, _):
            send[d] = source[jnp.maximum(asked(d), 0), :, lanes_of(r)]
            block_copy(send, recv, ssem, rsem, d, r).start()
            return 0

        lax.fori_loop(1, peers, one, 0)

    def fill_own(source, recv):
        @pl.when(r == 0)
        def _():
            block = jnp.maximum(asked(0), 0)
            for half in range(2):
                recv[0, half] = source[block, :, half * HALF : (half + 1) * HALF]

    def wait_blocks(m, send, recv, ssem, rsem):
        @pl.when(2 * m + r != 0)
        def _():
            for half in range(2):
                pltpu.make_async_remote_copy(
                    src_ref=send.at[0], dst_ref=recv.at[m, half],
                    send_sem=ssem.at[0], recv_sem=rsem.at[m, half],
                    device_id=twin, device_id_type=MESH,
                ).wait_recv()

    send_blocks(ft, fsend, frecv, fs, fr)
    send_blocks(yt.at[0], ysend.at[0], yrecv.at[0], ys.at[0], yr.at[0])
    fill_own(ft, frecv)

    def back_copy(it, m):
        return pltpu.make_async_remote_copy(
            src_ref=bsend.at[it, m], dst_ref=brecv.at[it, m],
            send_sem=bs.at[it, m], recv_sem=br.at[it, m],
            device_id={"blk": lax.rem(me - 2 * m - r + peers, peers), "rep": r},
            device_id_type=MESH,
        )

    def send_back(it, m):
        d = 2 * m + r
        keep = jnp.where(differ(d) > 0, 1.0, 0.0)
        y_a = (yt[it, jnp.maximum(own(d), 0)].astype(F32) * keep).astype(BF16)
        bsend[it, m] = mm(y_a, q[m], NN).astype(BF16)

        @pl.when(d != 0)
        def _():
            back_copy(it, m).start()

        @pl.when(d == 0)
        def _():
            brecv[it, m] = bsend[it, m]

    def make_tile(m, _):
        block = jnp.maximum(own(2 * m + r), 0)
        wait_blocks(m, fsend, frecv, fs, fr)
        right_sq = [
            jnp.sum(jnp.square(frecv[m, h].astype(F32)), axis=0, keepdims=True) * (1.0 / 16.0)
            for h in range(2)
        ]

        def chunk(p, _):
            at = pl.ds(pl.multiple_of(p * CHUNK, CHUNK), CHUNK)
            left = fn[block, at, :]
            left_sq = jnp.sum(jnp.square(left.astype(F32)), axis=1, keepdims=True) * 4.0
            for h in range(2):
                cross = mm(left, frecv[m, h], NN)
                dist = left_sq + right_sq[h]
                q[m, at, h * HALF : (h + 1) * HALF] = jnp.exp(cross - dist).astype(BF16)
            return 0

        lax.fori_loop(0, BS // CHUNK, chunk, 0)
        send_back(0, m)
        return 0

    lax.fori_loop(0, per, make_tile, 0)

    pl_r, pl_c = rows_cols((blocks * width, width))

    for it in range(ITERS):
        last = it == ITERS - 1
        fill_own(yt.at[it], yrecv.at[it])
        if it > 0:

            def back(m, _):
                send_back(it, m)
                return 0

            lax.fori_loop(0, per, back, 0)
        zt[...] = jnp.zeros_like(zt)

        def product(m, _):
            wait_blocks(m, ysend.at[it], yrecv.at[it], ys.at[it], yr.at[it])
            place = flags(pl_r == pl_c + own(2 * m + r) * width)
            for h in range(2):
                ypl[:, h * HALF : (h + 1) * HALF] = mm(place, yrecv[it, m, h], NN).astype(BF16)

            def chunk(p, _):
                at = pl.ds(pl.multiple_of(p * CHUNK, CHUNK), CHUNK)
                zt[:, at] += mm(ypl[...], q[m, at, :], NT)
                return 0

            lax.fori_loop(0, BS // CHUNK, chunk, 0)
            return 0

        lax.fori_loop(0, per, product, 0)

        def collect(m, _):
            d = 2 * m + r
            eb[m] = flags((pl_r == pl_c + asked(d) * width) & (asked(d) >= 0))

            @pl.when(d != 0)
            def _():
                back_copy(it, m).wait_recv()

            return 0

        lax.fori_loop(0, per, collect, 0)
        def swap(b):
            at = slice(b * width, (b + 1) * width)
            return pltpu.make_async_remote_copy(
                src_ref=zt.at[at, :], dst_ref=zx.at[it, at, :], send_sem=zsem_s.at[it, b],
                recv_sem=zsem_r.at[it, b], device_id=twin, device_id_type=MESH,
            )

        for b in range(blocks):
            at = slice(b * width, (b + 1) * width)
            total = zt[at, :]
            for m in range(per):
                total = total + mm(eb[m, at, :], brecv[it, m], NN)
            zt[at, :] = total
            swap(b).start()
        for b in range(blocks):
            at = slice(b * width, (b + 1) * width)
            swap(b).wait()
            zt[at, :] = (zt[at, :] + zx[it, at, :]) * scale[b]

        gram = jnp.zeros((2 * width, 2 * width), F32)
        for b in range(0, blocks, 2):
            w_t = zt[b * width : (b + 2) * width, :]
            gram = gram + mm(w_t, w_t, NT, HI)
        gram = gram[:width] + pltpu.roll(gram[width:], width, 1)
        low = rows_cols((half_w, 2 * width))[1] < width
        gx[it, me] = jnp.where(low, gram[:half_w], pltpu.roll(gram[half_w:], width, 1))

        def gram_copy(t, src):
            return pltpu.make_async_remote_copy(
                src_ref=gx.at[it, src], dst_ref=gx.at[it, src],
                send_sem=gs.at[it, t], recv_sem=gr.at[it, src],
                device_id={"blk": lax.rem(me + t, peers), "rep": r}, device_id_type=MESH,
            )

        def gram_send(t, _):
            gram_copy(t, me).start()
            return 0

        def gram_wait(t, _):
            gram_copy(t, lax.rem(me + t, peers)).wait_recv()
            return 0

        def gram_done(t, _):
            gram_copy(t, me).wait_send()
            return 0

        lax.fori_loop(1, peers, gram_send, 0)
        lax.fori_loop(1, peers, gram_wait, 0)
        gram = gx[it, 0]
        for t in range(1, peers):
            gram = gram + gx[it, t]
        gram = jnp.concatenate([gram, pltpu.roll(gram, width, 1)], axis=0)
        result = cholesky_and_inverse(gram * (1.0 / total_rows), width)

        inverse = pltpu.roll(result, width, 1)[:, :width]
        if last:
            for b in range(blocks // 2):
                at = pl.ds(pl.multiple_of((r * (blocks // 2) + b) * width, width), width)
                out[:, b * BS : (b + 1) * BS] = mm(inverse, zt[at, :], NN, HI)
            chol[...] = result
            l_r, l_c = rows_cols((width, 2 * width))
            factor[...] = mm(flags(l_r == l_c, F32), chol[...], NT, HI)
        else:
            for b in range(blocks):
                v_t = mm(inverse, zt[b * width : (b + 1) * width, :], NN, HI)
                yt[it + 1, b] = (v_t * scale[b]).astype(BF16)
            nxt = it + 1
            send_blocks(yt.at[nxt], ysend.at[nxt], yrecv.at[nxt], ys.at[nxt], yr.at[nxt])
        lax.fori_loop(1, peers, gram_done, 0)

    def blocks_done(d, _):
        block_copy(fsend, frecv, fs, fr, d, r).wait_send()
        for it in range(ITERS):
            block_copy(ysend.at[it], yrecv.at[it], ys.at[it], yr.at[it], d, r).wait_send()
        return 0

    lax.fori_loop(1, peers, blocks_done, 0)

    def info_done(t, _):
        info_copy(t, k).wait_send()
        return 0

    lax.fori_loop(1, devs, info_done, 0)

    def back_done(m, _):
        @pl.when(2 * m + r != 0)
        def _():
            for it in range(ITERS):
                back_copy(it, m).wait_send()

        return 0

    lax.fori_loop(0, per, back_done, 0)


def per_device(frames, degree, start, block_slot, pair_list, pair_count):
    peers = lax.axis_size("blk")
    local_rows, width = start.shape
    blocks = local_rows // BS
    slots = pair_list.shape[2]
    per = peers // 2
    devs = 2 * peers
    dma = pltpu.SemaphoreType.DMA
    vmem = pl.BlockSpec(memory_space=pltpu.VMEM)
    smem = pl.BlockSpec(memory_space=pltpu.SMEM)
    scratch = [
        pltpu.VMEM((devs, 1, 128), jnp.int32),
        pltpu.SMEM((devs, 1, 128), jnp.int32),
        pltpu.VMEM((blocks, width, BS), BF16),
        pltpu.VMEM((blocks, BS, width), BF16),
        pltpu.VMEM((ITERS, blocks, width, BS), BF16),
        pltpu.VMEM((blocks, 1, BS), F32),
        pltpu.VMEM((peers, width, HALF), BF16),
        pltpu.VMEM((per, 2, width, HALF), BF16),
        pltpu.VMEM((ITERS, peers, width, HALF), BF16),
        pltpu.VMEM((ITERS, per, 2, width, HALF), BF16),
        pltpu.VMEM((per, BS, BS), BF16),
        pltpu.VMEM((blocks * width, BS), BF16),
        pltpu.VMEM((blocks * width, BS), F32),
        pltpu.VMEM((ITERS, blocks * width, BS), F32),
        pltpu.VMEM((ITERS, per, width, BS), BF16),
        pltpu.VMEM((ITERS, per, width, BS), BF16),
        pltpu.VMEM((per, blocks * width, width), BF16),
        pltpu.VMEM((ITERS, peers, width // 2, 2 * width), F32),
        pltpu.VMEM((width, 2 * width), F32),
        dma((devs,)), dma((devs,)), dma,
        dma((peers,)), dma((per, 2)),
        dma((ITERS, peers)), dma((ITERS, per, 2)),
        dma((ITERS, per)), dma((ITERS, per)),
        dma((ITERS, blocks)), dma((ITERS, blocks)),
        dma((ITERS, peers)), dma((ITERS, peers)),
    ]
    out_t, factor = pl.pallas_call(
        functools.partial(kernel, peers, blocks, width, slots, local_rows * peers),
        out_shape=(
            jax.ShapeDtypeStruct((width, local_rows // 2), F32),
            jax.ShapeDtypeStruct((width, width), F32),
        ),
        in_specs=[vmem, vmem, vmem, smem, smem, smem],
        out_specs=(vmem, vmem),
        scratch_shapes=scratch,
        compiler_params=pltpu.CompilerParams(
            collective_id=0, has_side_effects=True, vmem_limit_bytes=56 * 1024 * 1024
        ),
    )(
        frames.T,
        degree.reshape(1, local_rows),
        start.T,
        block_slot,
        pair_list.reshape(-1),
        pair_count.reshape(-1),
    )
    return out_t.T, factor


def solution(mesh):
    placed = (
        P(("groups", "blk"), None),
        P(("groups", "blk")),
        P(("groups", "blk"), None),
        P("groups"),
        P(("groups", "blk"), "rep", None, None),
        P(("groups", "blk"), "rep"),
    )
    return jax.shard_map(
        per_device,
        mesh=mesh,
        in_specs=placed,
        out_specs=(P(("groups", "blk", "rep"), None), P("groups", None)),
        check_vma=False,
    )
```
